32 devices in a mesh: groups: 2 (over y), fibre: 4 (over z), tm: 2 (over x), freq: 2 (over core).
Axes of the slice: x: 2, y: 2, z: 4, core: 2. Of those that a mesh axis runs over, the one named last changes fastest.
Arguments:
- strain_rate: bfloat16 [8, 512, 1024], P(('fibre', 'tm'), 'groups'), parts along dimension 1, may hold values from -40 to 40
Outputs:
- correlations: float32 [64, 512, 401], P(('tm', 'freq'), ('groups', 'fibre')), parts along dimension 1
The draws below stay inside these ranges and needn't reach their ends.
There are 2 independent parts, one for each index of `groups`. The reference program is written for one: setup_inputs(seed, part) draws one part's arguments, and reference() takes and returns one part's arrays. A program takes and returns all parts, laid end to end along the dimension named above; each array names one. Nothing has to cross between parts.
All inputs are finite; a program needn't handle non-finite values.
Results may differ from the reference program's by a relative error of at most 0.0085.
Values may be sent and summed in bfloat16 or wider, within the bound.
A program may use at most 64 MiB of HBM per device.

```python
import math
import jax
import jax.numpy as jnp
from jax import lax

SEG_DEV = 1
SEG_LEN = 1024
FREQS = 256
OFFS = 64
LAGS = 401
SEGS = 8
CH = 256
N_FIBRE = 4
N_TM = 2


def draw_strain_rate(key, part):
    key = jax.random.fold_in(key, 7)
    noise_key, chan_key, seg_key = jax.random.split(key, 3)
    noise = jnp.clip(jax.random.normal(noise_key, (SEGS, CH, SEG_LEN + 2), jnp.float32), -4.0, 4.0)
    colored = noise[:, :, :-2] + noise[:, :, 1:-1] + noise[:, :, 2:]
    chan_gain = jnp.exp(jax.random.uniform(chan_key, (1, CH, 1), jnp.float32, math.log(0.3), math.log(3.0)))
    seg_gain = jnp.exp(jax.random.uniform(seg_key, (SEGS, 1, 1), jnp.float32, math.log(0.5), math.log(2.0)))
    field = colored * chan_gain * seg_gain
    return jnp.clip(field, -40.0, 40.0).astype(jnp.bfloat16)


def setup_inputs(seed: int = 0, part: int = 0) -> dict:
    seeds = jax.random.split(jax.random.key(seed), 2)
    own_keys = jax.random.split(jax.random.fold_in(seeds[1], part), 2)
    strain_rate = draw_strain_rate(jax.random.fold_in(jax.random.fold_in(seeds[1], part), 71), part)
    return dict(strain_rate=strain_rate)


water_level = 0.5

def forward_table(first_bin, bin_count, seg_length):
    sample_index = jnp.arange(seg_length, dtype=jnp.int32)
    bin_index = first_bin + jnp.arange(bin_count, dtype=jnp.int32)
    phase_index = sample_index[:, None] * bin_index[None, :] % seg_length
    angles = 2.0 * math.pi / seg_length * phase_index.astype(jnp.float32)
    hann_taper = 0.5 - 0.5 * jnp.cos(2.0 * math.pi / seg_length * sample_index.astype(jnp.float32))
    cosine = hann_taper[:, None] * jnp.cos(angles)
    sine_part = -hann_taper[:, None] * jnp.sin(angles)
    return jnp.concatenate([cosine, sine_part], axis=1).astype(jnp.bfloat16)

def inverse_table(first_bin, bin_count, lag_count, seg_length):
    bin_index = first_bin + jnp.arange(bin_count, dtype=jnp.int32)
    lag_index = jnp.arange(lag_count, dtype=jnp.int32) - (lag_count - 1) // 2
    phase_index = bin_index[:, None] * lag_index[None, :] % seg_length
    angles = 2.0 * math.pi / seg_length * phase_index.astype(jnp.float32)
    return jnp.concatenate([jnp.cos(angles), -jnp.sin(angles)], axis=0)

def reference(strain_rate):
    spectra = jnp.dot(strain_rate.reshape(SEGS * CH, SEG_LEN), forward_table(1, FREQS, SEG_LEN), preferred_element_type=jnp.float32).reshape(SEGS, CH, 2, FREQS)
    band_power = lax.optimization_barrier(jnp.sum(spectra * spectra, axis=(2, 3))) / FREQS
    water_floor = water_level * jnp.sqrt(band_power + 1e-06)
    amplitude = jnp.sqrt(spectra[:, :, 0] ** 2 + spectra[:, :, 1] ** 2)
    whitened = (spectra / jnp.maximum(amplitude, water_floor[:, :, None])[:, :, None, :]).astype(jnp.bfloat16)
    grouped = whitened.reshape(N_FIBRE, N_TM, SEG_DEV, CH, 2, FREQS)
    padded = jnp.pad(grouped, ((0, 0), (0, 0), (0, 0), (0, OFFS), (0, 0), (0, 0)))

    def one_offset(offset_now):
        partner = lax.dynamic_slice_in_dim(padded, offset_now.astype(jnp.int32), CH, axis=3)
        own_real = grouped[:, :, :, :, 0].astype(jnp.float32)
        own_imag = grouped[:, :, :, :, 1].astype(jnp.float32)
        other_real = partner[:, :, :, :, 0].astype(jnp.float32)
        other_imag = partner[:, :, :, :, 1].astype(jnp.float32)
        real_part = lax.optimization_barrier(jnp.sum(own_real * other_real + own_imag * other_imag, axis=(0, 2)))
        imag_part = lax.optimization_barrier(jnp.sum(own_imag * other_real - own_real * other_imag, axis=(0, 2)))
        group_sums = jnp.stack([real_part, imag_part], axis=2)
        rounded = lax.optimization_barrier(group_sums.astype(jnp.bfloat16)).astype(jnp.float32)
        return lax.optimization_barrier(jnp.sum(rounded, axis=0))
    stacked = lax.map(one_offset, 1 + jnp.arange(OFFS, dtype=jnp.int32))
    norm_factor = 1.0 / math.sqrt(SEGS * FREQS)
    correlations = jnp.dot(stacked.reshape(OFFS * CH, 2 * FREQS), inverse_table(1, FREQS, LAGS, SEG_LEN), precision=lax.Precision.HIGHEST, preferred_element_type=jnp.float32)
    return (correlations * norm_factor).reshape(OFFS, CH, LAGS)
```

```python
import functools
import math

import jax
import jax.numpy as jnp
import numpy as np
from jax import lax
from jax.experimental import pallas as pl
from jax.experimental.pallas import tpu as pltpu
from jax.sharding import PartitionSpec as P
import ml_dtypes

FREQS = 256
OFFS = 64
LAGS = 401
LANES = 128
MESH = pl.DeviceIdType.MESH

water_level = 0.5


def forward_table(seg_length):
    t = np.arange(seg_length)[:, None]
    j = np.arange(1, FREQS + 1)[None, :]
    angles = (2.0 * math.pi / seg_length) * (t * j % seg_length)
    taper = 0.5 - 0.5 * np.cos(2.0 * math.pi / seg_length * t)
    real = (taper * np.cos(angles)).astype(np.float32)
    imag = (-taper * np.sin(angles)).astype(np.float32)
    parts = []
    for h in range(FREQS // LANES):
        cols = slice(h * LANES, (h + 1) * LANES)
        parts += [real[:, cols], imag[:, cols]]
    return np.concatenate(parts, axis=1).astype(ml_dtypes.bfloat16)


def inverse_table(seg_length):
    j = np.arange(1, FREQS + 1)[:, None]
    lag = np.arange(LAGS)[None, :] - (LAGS - 1) // 2
    angles = (2.0 * math.pi / seg_length) * (j * lag % seg_length)
    real, imag = np.cos(angles).astype(np.float32), -np.sin(angles).astype(np.float32)
    parts = []
    for h in range(FREQS // LANES):
        rows = slice(h * LANES, (h + 1) * LANES)
        parts += [real[rows], imag[rows]]
    return np.concatenate(parts, axis=0).astype(ml_dtypes.bfloat16)


def gather_kernel(nf, nt, x_ref, table_ref, g_ref, white, send_sem, recv_sem, pair_send, pair_recv):
    fibre, tm, core = lax.axis_index("fibre"), lax.axis_index("tm"), lax.axis_index("freq")
    segs = nf * nt
    me = fibre * nt + tm
    sibling = {"freq": 1 - core}
    block = x_ref.shape[1] // nf
    rows = block + OFFS

    def device(other):
        return {"fibre": lax.div(other, nt), "tm": lax.rem(other, nt)}

    barrier = pltpu.get_barrier_semaphore()
    pl.semaphore_signal(barrier, inc=1, device_id=sibling, device_id_type=MESH)

    def greet(i, _):
        pl.semaphore_signal(
            barrier, inc=1, device_id=device(lax.rem(me + i, segs)), device_id_type=MESH
        )
        return 0

    lax.fori_loop(1, segs, greet, 0)

    chans = x_ref.shape[1]
    step = 128

    def whiten(i, _):
        here = pl.ds(pl.multiple_of(i * step, step), step)
        spectra = jnp.dot(x_ref[0, here, :], table_ref[...], preferred_element_type=jnp.float32)
        squares = spectra * spectra
        power = jnp.sum(squares, axis=1, keepdims=True) * (1.0 / FREQS)
        floor = (power + 1e-06) * (water_level * water_level)
        for h in range(FREQS // LANES):
            re = slice(2 * h * LANES, (2 * h + 1) * LANES)
            im = slice((2 * h + 1) * LANES, (2 * h + 2) * LANES)
            scale = lax.rsqrt(jnp.maximum(squares[:, re] + squares[:, im], floor))
            white[h, here, 0:LANES] = (spectra[:, re] * scale).astype(jnp.bfloat16)
            white[h, here, LANES : 2 * LANES] = (spectra[:, im] * scale).astype(jnp.bfloat16)
        return 0

    lax.fori_loop(0, chans // step, whiten, 0, unroll=chans <= 512)
    white[:, chans:, :] = jnp.zeros((2, OFFS, 2 * LANES), jnp.bfloat16)

    pl.semaphore_wait(barrier, segs)

    def outgoing(i):
        other = lax.rem(me + i, segs)
        first = pl.multiple_of(lax.div(other, nt) * block, block)
        return pltpu.make_async_remote_copy(
            src_ref=white.at[core, pl.ds(first, rows)],
            dst_ref=g_ref.at[me, core],
            send_sem=send_sem.at[other],
            recv_sem=recv_sem.at[me],
            device_id=device(other),
            device_id_type=MESH,
        )

    def incoming(s):
        return pltpu.make_async_remote_copy(
            src_ref=white.at[core, pl.ds(0, rows)],
            dst_ref=g_ref.at[s, core],
            send_sem=send_sem.at[s],
            recv_sem=recv_sem.at[s],
            device_id=device(s),
            device_id_type=MESH,
        )

    def across(s, half):
        return pltpu.make_async_remote_copy(
            src_ref=g_ref.at[s, half],
            dst_ref=g_ref.at[s, half],
            send_sem=pair_send.at[s],
            recv_sem=pair_recv.at[s],
            device_id=sibling,
            device_id_type=MESH,
        )

    def start(i, _):
        outgoing(i).start()
        return 0

    lax.fori_loop(1, segs, start, 0)

    own = pl.ds(pl.multiple_of(fibre * block, block), rows)
    g_ref[me] = white[:, own, :]

    def forward(i, _):
        s = lax.rem(me + segs - i, segs)
        incoming(s).wait_recv()
        across(s, core).start()
        return 0

    lax.fori_loop(1, segs, forward, 0)

    def finish(i, _):
        s = lax.rem(me + segs - i, segs)
        across(s, 1 - core).wait_recv()
        across(s, core).wait_send()
        outgoing(i).wait_send()
        return 0

    lax.fori_loop(1, segs, finish, 0)


def cross_kernel(segs, group, block, norm, g_ref, inverse_ref, out_ref, right, stacked):
    step = pl.program_id(0)
    halves = FREQS // LANES
    share = group * pl.num_programs(0)
    place = lax.axis_index("tm") * lax.axis_size("freq") + lax.axis_index("freq")
    first = pl.multiple_of(place * share, 8)

    @pl.when(step == 0)
    def _():
        def widen(s, _):
            for h in range(halves):
                for p in range(2):
                    cols = slice(p * LANES, (p + 1) * LANES)
                    right[s, 2 * h + p] = g_ref[s, h, :, cols].astype(jnp.float32)
            return 0

        lax.fori_loop(0, segs, widen, 0)

    base = first + step * group + 1

    def tile(r, _):
        here = pl.ds(pl.multiple_of(r * 8, 8), 8)
        for h in range(halves):
            real = [jnp.zeros((8, LANES), jnp.float32)] * group
            imag = [jnp.zeros((8, LANES), jnp.float32)] * group

            def add(s, real, imag):
                a0, a1 = right[s, 2 * h, here, :], right[s, 2 * h + 1, here, :]
                for k in range(group):
                    there = pl.ds(base + (r * 8 + k), 8)
                    b0, b1 = right[s, 2 * h, there, :], right[s, 2 * h + 1, there, :]
                    real[k] = real[k] + (a0 * b0 + a1 * b1)
                    imag[k] = imag[k] + (a1 * b0 - a0 * b1)

            if segs <= 16:
                for s in range(segs):
                    add(s, real, imag)
            else:

                def body(s, carry):
                    real, imag = list(carry[0]), list(carry[1])
                    add(s, real, imag)
                    return tuple(real), tuple(imag)

                real, imag = lax.fori_loop(0, segs, body, (tuple(real), tuple(imag)))
            for k in range(group):
                at = pl.ds(pl.multiple_of(k * block + r * 8, 8), 8)
                stacked[at, 2 * h * LANES : (2 * h + 1) * LANES] = real[k]
                stacked[at, (2 * h + 1) * LANES : (2 * h + 2) * LANES] = imag[k]
        return 0

    lax.fori_loop(0, block // 8, tile, 0)
    terms = jnp.dot(
        stacked[...].astype(jnp.bfloat16), inverse_ref[...], preferred_element_type=jnp.float32
    )
    out_ref[...] = (terms * norm).reshape(group, block, LAGS)


def local(nf, nt, nq, strain_rate):
    _, chans, seg_length = strain_rate.shape
    segs = nf * nt
    block = chans // nf
    rows = block + OFFS
    share = OFFS // (nt * nq)
    group = 4
    vmem = pl.BlockSpec(memory_space=pltpu.VMEM)
    gathered = pl.pallas_call(
        functools.partial(gather_kernel, nf, nt),
        out_shape=jax.ShapeDtypeStruct((segs, 2, rows, 2 * LANES), jnp.bfloat16),
        in_specs=[vmem, vmem],
        out_specs=vmem,
        scratch_shapes=[
            pltpu.VMEM((2, chans + OFFS, 2 * LANES), jnp.bfloat16),
            pltpu.SemaphoreType.DMA((segs,)),
            pltpu.SemaphoreType.DMA((segs,)),
            pltpu.SemaphoreType.DMA((segs,)),
            pltpu.SemaphoreType.DMA((segs,)),
        ],
        compiler_params=pltpu.CompilerParams(
            collective_id=0, has_side_effects=True, vmem_limit_bytes=48 << 20
        ),
    )(strain_rate, jnp.asarray(forward_table(seg_length)))
    norm = 1.0 / math.sqrt(segs * FREQS)
    return pl.pallas_call(
        functools.partial(cross_kernel, segs, group, block, norm),
        grid=(share // group,),
        out_shape=jax.ShapeDtypeStruct((share, block, LAGS), jnp.float32),
        in_specs=[vmem, vmem],
        out_specs=pl.BlockSpec((group, block, LAGS), lambda i: (i, 0, 0)),
        scratch_shapes=[
            pltpu.VMEM((segs, 4, rows, LANES), jnp.float32),
            pltpu.VMEM((group * block, 2 * FREQS), jnp.float32),
        ],
        compiler_params=pltpu.CompilerParams(
            dimension_semantics=("arbitrary",),
            vmem_limit_bytes=(32 << 20) if segs <= 32 else (60 << 20),
        ),
    )(gathered, jnp.asarray(inverse_table(seg_length)))


def solution(mesh):
    sizes = mesh.shape
    return jax.shard_map(
        functools.partial(local, sizes["fibre"], sizes["tm"], sizes["freq"]),
        mesh=mesh,
        in_specs=(P(("fibre", "tm"), "groups", None),),
        out_specs=P(("tm", "freq"), ("groups", "fibre"), None),
        check_vma=False,
    )
```

```python
import functools
import math

import jax
import jax.numpy as jnp
import numpy as np
from jax import lax
from jax.experimental import pallas as pl
from jax.experimental.pallas import tpu as pltpu
from jax.sharding import PartitionSpec as P
import ml_dtypes

FREQS = 256
OFFS = 64
LAGS = 401
LANES = 128
MESH = pl.DeviceIdType.MESH

water_level = 0.5


def forward_table(seg_length):
    t = np.arange(seg_length)[:, None]
    j = np.arange(1, FREQS + 1)[None, :]
    angles = (2.0 * math.pi / seg_length) * (t * j % seg_length)
    taper = 0.5 - 0.5 * np.cos(2.0 * math.pi / seg_length * t)
    real = (taper * np.cos(angles)).astype(np.float32)
    imag = (-taper * np.sin(angles)).astype(np.float32)
    parts = []
    for h in range(FREQS // LANES):
        cols = slice(h * LANES, (h + 1) * LANES)
        parts += [real[:, cols], imag[:, cols]]
    return np.concatenate(parts, axis=1).astype(ml_dtypes.bfloat16)


def inverse_table(seg_length):
    j = np.arange(1, FREQS + 1)[:, None]
    lag = np.arange(LAGS)[None, :] - (LAGS - 1) // 2
    angles = (2.0 * math.pi / seg_length) * (j * lag % seg_length)
    real, imag = np.cos(angles).astype(np.float32), -np.sin(angles).astype(np.float32)
    parts = []
    for h in range(FREQS // LANES):
        rows = slice(h * LANES, (h + 1) * LANES)
        parts += [real[rows], imag[rows]]
    return np.concatenate(parts, axis=0).astype(ml_dtypes.bfloat16)


def gather_kernel(
    nf, nt, x_hbm, table_hbm, g_ref, x_ref, table_ref, white,
    load_sem, fibre_send, tm_send, recv_sem, pair_send, pair_recv,
):
    fibre, tm, core = lax.axis_index("fibre"), lax.axis_index("tm"), lax.axis_index("freq")
    me = fibre * nt + tm
    sibling = {"freq": 1 - core}
    chans = x_ref.shape[0]
    block = chans // nf
    rows = block + OFFS
    step = 128
    steps = chans // step
    depth = table_ref.shape[0] // 4

    def load_x(i):
        here = pl.ds(pl.multiple_of(i * step, step), step)
        return pltpu.make_async_copy(x_hbm.at[0, here], x_ref.at[here], load_sem.at[4 + i])

    def load_table(i):
        here = pl.ds(i * depth, depth)
        return pltpu.make_async_copy(table_hbm.at[here], table_ref.at[here], load_sem.at[i])

    for i in range(4):
        load_table(i).start()
    for i in range(steps):
        load_x(i).start()

    barrier = pltpu.get_barrier_semaphore()
    pl.semaphore_signal(barrier, inc=1, device_id=sibling, device_id_type=MESH)
    for i in range(1, nf):
        to = {"fibre": lax.rem(fibre + i, nf)}
        pl.semaphore_signal(barrier, inc=1, device_id=to, device_id_type=MESH)
    for i in range(1, nt):
        to = {"tm": lax.rem(tm + i, nt)}
        pl.semaphore_signal(barrier, inc=1, device_id=to, device_id_type=MESH)

    for i in range(4):
        load_table(i).wait()

    def whiten(i, _):
        here = pl.ds(pl.multiple_of(i * step, step), step)
        load_x(i).wait()
        spectra = jnp.dot(x_ref[here, :], table_ref[...], preferred_element_type=jnp.float32)
        squares = spectra * spectra
        power = jnp.sum(squares, axis=1, keepdims=True) * (1.0 / FREQS)
        floor = (power + 1e-06) * (water_level * water_level)
        for h in range(FREQS // LANES):
            re = slice(2 * h * LANES, (2 * h + 1) * LANES)
            im = slice((2 * h + 1) * LANES, (2 * h + 2) * LANES)
            scale = lax.rsqrt(jnp.maximum(squares[:, re] + squares[:, im], floor))
            white[h, here, 0:LANES] = (spectra[:, re] * scale).astype(jnp.bfloat16)
            white[h, here, LANES : 2 * LANES] = (spectra[:, im] * scale).astype(jnp.bfloat16)
        return 0

    white[:, chans:, :] = jnp.zeros((2, OFFS, 2 * LANES), jnp.bfloat16)
    lax.fori_loop(0, steps, whiten, 0, unroll=steps <= 4)

    pl.semaphore_wait(barrier, nf + nt - 1)

    def own_rows(f):
        return pl.ds(pl.multiple_of(f * block, block), rows)

    def along_fibre(i):
        f = lax.rem(fibre + i, nf)
        return pltpu.make_async_remote_copy(
            src_ref=white.at[core, own_rows(f)],
            dst_ref=g_ref.at[me, core],
            send_sem=fibre_send.at[i],
            recv_sem=recv_sem.at[me],
            device_id={"fibre": f},
            device_id_type=MESH,
        )

    def along_tm(j, i):
        s = lax.rem(fibre + nf - j, nf) * nt + tm
        own = isinstance(j, int) and j == 0
        return pltpu.make_async_remote_copy(
            src_ref=white.at[core, own_rows(fibre)] if own else g_ref.at[s, core],
            dst_ref=g_ref.at[s, core],
            send_sem=tm_send.at[j, i],
            recv_sem=recv_sem.at[s],
            device_id={"tm": lax.rem(tm + i, nt)},
            device_id_type=MESH,
        )

    def arrived(s):
        return pltpu.make_async_remote_copy(
            src_ref=g_ref.at[s, core],
            dst_ref=g_ref.at[s, core],
            send_sem=pair_send.at[s],
            recv_sem=recv_sem.at[s],
            device_id=sibling,
            device_id_type=MESH,
        )

    def across(s, half):
        return pltpu.make_async_remote_copy(
            src_ref=g_ref.at[s, half],
            dst_ref=g_ref.at[s, half],
            send_sem=pair_send.at[s],
            recv_sem=pair_recv.at[s],
            device_id=sibling,
            device_id_type=MESH,
        )

    def loop(low, high, body):
        if high - low <= 8:
            for i in range(low, high):
                body(i)
        else:
            lax.fori_loop(low, high, lambda i, _: (body(i), 0)[1], 0)

    for i in range(1, nt):
        along_tm(0, i).start()
    loop(1, nf, lambda i: along_fibre(i).start())
    g_ref[me] = white[:, own_rows(fibre), :]

    def column(j):
        s = lax.rem(fibre + nf - j, nf) * nt + tm
        arrived(s).wait_recv()
        for i in range(1, nt):
            along_tm(j, i).start()
        across(s, core).start()

    loop(1, nf, column)

    def others(j):
        for i in range(1, nt):
            s = lax.rem(fibre + nf - j, nf) * nt + lax.rem(tm + nt - i, nt)
            arrived(s).wait_recv()
            across(s, core).start()

    loop(0, nf, others)

    def finish(j):
        for i in range(nt):
            s = lax.rem(fibre + nf - j, nf) * nt + lax.rem(tm + nt - i, nt)
            if i > 0 or not (isinstance(j, int) and j == 0):
                across(s, 1 - core).wait_recv()
                across(s, core).wait_send()
        for i in range(1, nt):
            along_tm(j, i).wait_send()
        if not (isinstance(j, int) and j == 0):
            along_fibre(j).wait_send()

    finish(0)
    loop(1, nf, finish)


def cross_kernel(segs, group, block, norm, g_ref, inverse_ref, out_ref, right, stacked):
    step = pl.program_id(0)
    halves = FREQS // LANES
    share = group * pl.num_programs(0)
    place = lax.axis_index("tm") * lax.axis_size("freq") + lax.axis_index("freq")
    first = pl.multiple_of(place * share, 8)

    @pl.when(step == 0)
    def _():
        def widen(s, _):
            for h in range(halves):
                for p in range(2):
                    cols = slice(p * LANES, (p + 1) * LANES)
                    right[s, 2 * h + p] = g_ref[s, h, :, cols].astype(jnp.float32)
            return 0

        lax.fori_loop(0, segs, widen, 0)

    base = first + step * group + 1

    def tile(r, _):
        here = pl.ds(pl.multiple_of(r * 8, 8), 8)
        for h in range(halves):
            real = [jnp.zeros((8, LANES), jnp.float32)] * group
            imag = [jnp.zeros((8, LANES), jnp.float32)] * group

            def add(s, real, imag):
                a0, a1 = right[s, 2 * h, here, :], right[s, 2 * h + 1, here, :]
                for k in range(group):
                    there = pl.ds(base + (r * 8 + k), 8)
                    b0, b1 = right[s, 2 * h, there, :], right[s, 2 * h + 1, there, :]
                    real[k] = real[k] + (a0 * b0 + a1 * b1)
                    imag[k] = imag[k] + (a1 * b0 - a0 * b1)

            if segs <= 16:
                for s in range(segs):
                    add(s, real, imag)
            else:

                def body(s, carry):
                    real, imag = list(carry[0]), list(carry[1])
                    add(s, real, imag)
                    return tuple(real), tuple(imag)

                real, imag = lax.fori_loop(0, segs, body, (tuple(real), tuple(imag)))
            for k in range(group):
                at = pl.ds(pl.multiple_of(k * block + r * 8, 8), 8)
                stacked[at, 2 * h * LANES : (2 * h + 1) * LANES] = real[k]
                stacked[at, (2 * h + 1) * LANES : (2 * h + 2) * LANES] = imag[k]
        return 0

    lax.fori_loop(0, block // 8, tile, 0)
    terms = jnp.dot(
        stacked[...].astype(jnp.bfloat16), inverse_ref[...], preferred_element_type=jnp.float32
    )
    out_ref[...] = (terms * norm).reshape(group, block, LAGS)


def local(nf, nt, nq, strain_rate):
    _, chans, seg_length = strain_rate.shape
    segs = nf * nt
    block = chans // nf
    rows = block + OFFS
    share = OFFS // (nt * nq)
    group = 4
    vmem = pl.BlockSpec(memory_space=pltpu.VMEM)
    gathered = pl.pallas_call(
        functools.partial(gather_kernel, nf, nt),
        out_shape=jax.ShapeDtypeStruct((segs, 2, rows, 2 * LANES), jnp.bfloat16),
        in_specs=[pl.BlockSpec(memory_space=pl.ANY)] * 2,
        out_specs=vmem,
        scratch_shapes=[
            pltpu.VMEM((chans, seg_length), jnp.bfloat16),
            pltpu.VMEM((seg_length, 2 * FREQS), jnp.bfloat16),
            pltpu.VMEM((2, chans + OFFS, 2 * LANES), jnp.bfloat16),
            pltpu.SemaphoreType.DMA((4 + chans // 128,)),
            pltpu.SemaphoreType.DMA((nf,)),
            pltpu.SemaphoreType.DMA((nf, nt)),
            pltpu.SemaphoreType.DMA((segs,)),
            pltpu.SemaphoreType.DMA((segs,)),
            pltpu.SemaphoreType.DMA((segs,)),
        ],
        compiler_params=pltpu.CompilerParams(
            collective_id=0, has_side_effects=True, vmem_limit_bytes=48 << 20
        ),
    )(strain_rate, jnp.asarray(forward_table(seg_length)))
    norm = 1.0 / math.sqrt(segs * FREQS)
    return pl.pallas_call(
        functools.partial(cross_kernel, segs, group, block, norm),
        grid=(share // group,),
        out_shape=jax.ShapeDtypeStruct((share, block, LAGS), jnp.float32),
        in_specs=[vmem, vmem],
        out_specs=pl.BlockSpec((group, block, LAGS), lambda i: (i, 0, 0)),
        scratch_shapes=[
            pltpu.VMEM((segs, 4, rows, LANES), jnp.float32),
            pltpu.VMEM((group * block, 2 * FREQS), jnp.float32),
        ],
        compiler_params=pltpu.CompilerParams(
            dimension_semantics=("arbitrary",),
            vmem_limit_bytes=(32 << 20) if segs <= 32 else (60 << 20),
        ),
    )(gathered, jnp.asarray(inverse_table(seg_length)))


def solution(mesh):
    sizes = mesh.shape
    return jax.shard_map(
        functools.partial(local, sizes["fibre"], sizes["tm"], sizes["freq"]),
        mesh=mesh,
        in_specs=(P(("fibre", "tm"), "groups", None),),
        out_specs=P(("tm", "freq"), ("groups", "fibre"), None),
        check_vma=False,
    )
```

```python
import functools
import math

import jax
import jax.numpy as jnp
import numpy as np
from jax import lax
from jax.experimental import pallas as pl
from jax.experimental.pallas import tpu as pltpu
from jax.sharding import PartitionSpec as P
import ml_dtypes

FREQS = 256
OFFS = 64
LAGS = 401
LANES = 128
MESH = pl.DeviceIdType.MESH

water_level = 0.5


def forward_table(seg_length):
    t = np.arange(seg_length)[:, None]
    j = np.arange(1, FREQS + 1)[None, :]
    angles = (2.0 * math.pi / seg_length) * (t * j % seg_length)
    taper = 0.5 - 0.5 * np.cos(2.0 * math.pi / seg_length * t)
    real = (taper * np.cos(angles)).astype(np.float32)
    imag = (-taper * np.sin(angles)).astype(np.float32)
    parts = []
    for h in range(FREQS // LANES):
        cols = slice(h * LANES, (h + 1) * LANES)
        parts += [real[:, cols], imag[:, cols]]
    return np.concatenate(parts, axis=1).astype(ml_dtypes.bfloat16)


def inverse_table(seg_length):
    j = np.arange(1, FREQS + 1)[:, None]
    lag = np.arange(LAGS)[None, :] - (LAGS - 1) // 2
    angles = (2.0 * math.pi / seg_length) * (j * lag % seg_length)
    real, imag = np.cos(angles).astype(np.float32), -np.sin(angles).astype(np.float32)
    parts = []
    for h in range(FREQS // LANES):
        rows = slice(h * LANES, (h + 1) * LANES)
        parts += [real[rows], imag[rows]]
    return np.concatenate(parts, axis=0).astype(ml_dtypes.bfloat16)


def accumulate(load, spectra, acc, count, first, share, block, fresh):
    halves = FREQS // LANES
    for n in range(count):
        for h in range(halves):
            wide = load(n, h).astype(jnp.float32)
            spectra[n, 2 * h] = wide[:, :LANES]
            spectra[n, 2 * h + 1] = wide[:, LANES:]

    def tile(r, _):
        here = pl.ds(pl.multiple_of(r * 8, 8), 8)
        for h in range(halves):
            re = slice(2 * h * LANES, (2 * h + 1) * LANES)
            im = slice((2 * h + 1) * LANES, (2 * h + 2) * LANES)
            a0 = [spectra[n, 2 * h, here, :] for n in range(count)]
            a1 = [spectra[n, 2 * h + 1, here, :] for n in range(count)]
            for k in range(share):
                at = pl.ds(pl.multiple_of(k * block + r * 8, 8), 8)
                there = pl.ds(first + (r * 8 + k + 1), 8)
                real = imag = None
                for n in range(count):
                    b0, b1 = spectra[n, 2 * h, there, :], spectra[n, 2 * h + 1, there, :]
                    x, y = a0[n] * b0 + a1[n] * b1, a1[n] * b0 - a0[n] * b1
                    real = x if real is None else real + x
                    imag = y if imag is None else imag + y
                acc[at, re] = real if fresh else acc[at, re] + real
                acc[at, im] = imag if fresh else acc[at, im] + imag
        return 0

    lax.fori_loop(0, block // 8, tile, 0)


def stack_kernel(
    nf, nt, nq, x_hbm, table_hbm, acc, x_ref, table_ref, white, g_ref, spectra_ref,
    load_sem, fibre_send, tm_send, recv_sem, pair_send, pair_recv,
):
    fibre, tm, core = lax.axis_index("fibre"), lax.axis_index("tm"), lax.axis_index("freq")
    me = fibre * nt + tm
    sibling = {"freq": 1 - core}
    chans = x_ref.shape[0]
    block = chans // nf
    rows = block + OFFS
    chunks = 2
    part = rows // chunks
    step = 128
    steps = chans // step
    depth = table_ref.shape[0] // 4

    def load_x(i):
        here = pl.ds(pl.multiple_of(i * step, step), step)
        return pltpu.make_async_copy(x_hbm.at[0, here], x_ref.at[here], load_sem.at[4 + i])

    def load_table(i):
        here = pl.ds(i * depth, depth)
        return pltpu.make_async_copy(table_hbm.at[here], table_ref.at[here], load_sem.at[i])

    for i in range(4):
        load_table(i).start()
    for i in range(steps):
        load_x(i).start()

    barrier = pltpu.get_barrier_semaphore()
    pl.semaphore_signal(barrier, inc=1, device_id=sibling, device_id_type=MESH)
    for i in range(1, nf):
        to = {"fibre": lax.rem(fibre + i, nf)}
        pl.semaphore_signal(barrier, inc=1, device_id=to, device_id_type=MESH)
    for i in range(1, nt):
        to = {"tm": lax.rem(tm + i, nt)}
        pl.semaphore_signal(barrier, inc=1, device_id=to, device_id_type=MESH)

    for i in range(4):
        load_table(i).wait()

    def whiten(i, _):
        here = pl.ds(pl.multiple_of(i * step, step), step)
        load_x(i).wait()
        spectra = jnp.dot(x_ref[here, :], table_ref[...], preferred_element_type=jnp.float32)
        squares = spectra * spectra
        power = jnp.sum(squares, axis=1, keepdims=True) * (1.0 / FREQS)
        floor = (power + 1e-06) * (water_level * water_level)
        for h in range(FREQS // LANES):
            re = slice(2 * h * LANES, (2 * h + 1) * LANES)
            im = slice((2 * h + 1) * LANES, (2 * h + 2) * LANES)
            scale = lax.rsqrt(jnp.maximum(squares[:, re] + squares[:, im], floor))
            white[h, here, 0:LANES] = (spectra[:, re] * scale).astype(jnp.bfloat16)
            white[h, here, LANES : 2 * LANES] = (spectra[:, im] * scale).astype(jnp.bfloat16)
        return 0

    white[:, chans:, :] = jnp.zeros((2, OFFS, 2 * LANES), jnp.bfloat16)
    lax.fori_loop(0, steps, whiten, 0, unroll=steps <= 4)

    pl.semaphore_wait(barrier, nf + nt - 1)

    def rows_of(f, c):
        return pl.ds(pl.multiple_of(f * block + c * part, 16), part)

    def landing(s, c):
        return g_ref.at[s, core, pl.ds(c * part, part)]

    def along_fibre(f, c):
        return pltpu.make_async_remote_copy(
            src_ref=white.at[core, rows_of(f, c)],
            dst_ref=landing(me, c),
            send_sem=fibre_send.at[f, c],
            recv_sem=recv_sem.at[me, c],
            device_id={"fibre": f},
            device_id_type=MESH,
        )

    def along_tm(f, i, c, own=False):
        s = f * nt + tm
        return pltpu.make_async_remote_copy(
            src_ref=white.at[core, rows_of(fibre, c)] if own else landing(s, c),
            dst_ref=landing(s, c),
            send_sem=tm_send.at[f, i, c],
            recv_sem=recv_sem.at[s, c],
            device_id={"tm": lax.rem(tm + i, nt)},
            device_id_type=MESH,
        )

    def arrived(s, c):
        return pltpu.make_async_remote_copy(
            src_ref=landing(s, c),
            dst_ref=landing(s, c),
            send_sem=pair_send.at[s],
            recv_sem=recv_sem.at[s, c],
            device_id=sibling,
            device_id_type=MESH,
        )

    def across(s, half):
        return pltpu.make_async_remote_copy(
            src_ref=g_ref.at[s, half],
            dst_ref=g_ref.at[s, half],
            send_sem=pair_send.at[s],
            recv_sem=pair_recv.at[s],
            device_id=sibling,
            device_id_type=MESH,
        )

    def loop(low, high, body):
        if high - low <= 8:
            for i in range(low, high):
                body(i)
        else:
            lax.fori_loop(low, high, lambda i, _: (body(i), 0)[1], 0)

    def nearest_first(body):
        def at_distance(d):
            for f in (fibre + d, fibre - d):
                pl.when(jnp.logical_and(f >= 0, f < nf))(functools.partial(body, f))

        loop(1, nf, at_distance)

    for c in range(chunks):
        for i in range(1, nt):
            along_tm(fibre, i, c, own=True).start()

    @nearest_first
    def _(f):
        for c in range(chunks):
            along_fibre(f, c).start()

    g_ref[me] = jnp.stack(
        [white[h, pl.ds(pl.multiple_of(fibre * block, 16), rows), :] for h in range(2)]
    )

    @nearest_first
    def _(f):
        s = f * nt + tm
        for c in range(chunks):
            arrived(s, c).wait_recv()
            for i in range(1, nt):
                along_tm(f, i, c).start()
        across(s, core).start()

    share = acc.shape[0] // block
    place = tm * nq + core
    first = place * share

    @nearest_first
    def _(f):
        across(f * nt + tm, 1 - core).wait_recv()

    def add(batch, index, fresh):
        def load(n, h):
            return g_ref[index(n), h]

        accumulate(load, spectra_ref, acc, batch, first, share, block, fresh)

    batch = math.gcd(nf, 4)
    add(batch, lambda n: n * nt + tm, True)
    if nf > batch:
        loop(1, nf // batch, lambda i: add(batch, lambda n: (i * batch + n) * nt + tm, False))

    def pass_on(f):
        for i in range(1, nt):
            s = f * nt + lax.rem(tm + i, nt)
            for c in range(chunks):
                arrived(s, c).wait_recv()
            across(s, core).start()

    pass_on(fibre)
    nearest_first(pass_on)
    for i in range(1, nt):
        other = lax.rem(tm + i, nt)

        def part_of(b):
            for n in range(batch):
                across((b * batch + n) * nt + other, 1 - core).wait_recv()
            add(batch, lambda n: (b * batch + n) * nt + other, False)

        loop(0, nf // batch, part_of)

    for i in range(1, nt):
        across(fibre * nt + lax.rem(tm + i, nt), core).wait_send()
        for c in range(chunks):
            along_tm(fibre, i, c, own=True).wait_send()

    @nearest_first
    def _(f):
        for c in range(chunks):
            along_fibre(f, c).wait_send()
        for i in range(nt):
            across(f * nt + lax.rem(tm + i, nt), core).wait_send()
            if i > 0:
                for c in range(chunks):
                    along_tm(f, i, c).wait_send()


def lag_kernel(norm, stacked_ref, inverse_ref, out_ref):
    terms = jnp.dot(
        stacked_ref[...].astype(jnp.bfloat16), inverse_ref[...], preferred_element_type=jnp.float32
    )
    out_ref[...] = (terms * norm).reshape(out_ref.shape)


def local(nf, nt, nq, strain_rate):
    _, chans, seg_length = strain_rate.shape
    segs = nf * nt
    block = chans // nf
    rows = block + OFFS
    share = OFFS // (nt * nq)
    group = 4
    vmem = pl.BlockSpec(memory_space=pltpu.VMEM)
    stacked = pl.pallas_call(
        functools.partial(stack_kernel, nf, nt, nq),
        out_shape=jax.ShapeDtypeStruct((share * block, 2 * FREQS), jnp.float32),
        in_specs=[pl.BlockSpec(memory_space=pltpu.HBM)] * 2,
        out_specs=vmem,
        scratch_shapes=[
            pltpu.VMEM((chans, seg_length), jnp.bfloat16),
            pltpu.VMEM((seg_length, 2 * FREQS), jnp.bfloat16),
            pltpu.VMEM((2, chans + OFFS, 2 * LANES), jnp.bfloat16),
            pltpu.VMEM((segs, 2, rows, 2 * LANES), jnp.bfloat16),
            pltpu.VMEM((math.gcd(nf, 4), 4, rows, LANES), jnp.float32),
            pltpu.SemaphoreType.DMA((4 + chans // 128,)),
            pltpu.SemaphoreType.DMA((nf, 2)),
            pltpu.SemaphoreType.DMA((nf, nt, 2)),
            pltpu.SemaphoreType.DMA((segs, 2)),
            pltpu.SemaphoreType.DMA((segs,)),
            pltpu.SemaphoreType.DMA((segs,)),
        ],
        compiler_params=pltpu.CompilerParams(
            collective_id=0, has_side_effects=True, vmem_limit_bytes=60 << 20
        ),
    )(strain_rate, jnp.asarray(forward_table(seg_length)))
    norm = 1.0 / math.sqrt(segs * FREQS)
    return pl.pallas_call(
        functools.partial(lag_kernel, norm),
        grid=(share // group,),
        out_shape=jax.ShapeDtypeStruct((share, block, LAGS), jnp.float32),
        in_specs=[
            pl.BlockSpec((group * block, 2 * FREQS), lambda i: (i, 0)),
            pl.BlockSpec((2 * FREQS, LAGS), lambda i: (0, 0)),
        ],
        out_specs=pl.BlockSpec((group, block, LAGS), lambda i: (i, 0, 0)),
        compiler_params=pltpu.CompilerParams(dimension_semantics=("arbitrary",)),
    )(stacked, jnp.asarray(inverse_table(seg_length)))


def solution(mesh):
    sizes = mesh.shape
    return jax.shard_map(
        functools.partial(local, sizes["fibre"], sizes["tm"], sizes["freq"]),
        mesh=mesh,
        in_specs=(P(("fibre", "tm"), "groups", None),),
        out_specs=P(("tm", "freq"), ("groups", "fibre"), None),
        check_vma=False,
    )
```

```python
import functools
import math

import jax
import jax.numpy as jnp
import numpy as np
from jax import lax
from jax.experimental import pallas as pl
from jax.experimental.pallas import tpu as pltpu
from jax.sharding import PartitionSpec as P
import ml_dtypes

FREQS = 256
OFFS = 64
LAGS = 401
LANES = 128
MESH = pl.DeviceIdType.MESH

water_level = 0.5


def forward_table(seg_length):
    t = np.arange(seg_length)[:, None]
    j = np.arange(1, FREQS + 1)[None, :]
    angles = (2.0 * math.pi / seg_length) * (t * j % seg_length)
    taper = 0.5 - 0.5 * np.cos(2.0 * math.pi / seg_length * t)
    real = (taper * np.cos(angles)).astype(np.float32)
    imag = (-taper * np.sin(angles)).astype(np.float32)
    parts = []
    for h in range(FREQS // LANES):
        cols = slice(h * LANES, (h + 1) * LANES)
        parts += [real[:, cols], imag[:, cols]]
    return np.concatenate(parts, axis=1).astype(ml_dtypes.bfloat16)


def inverse_table(seg_length):
    j = np.arange(1, FREQS + 1)[:, None]
    lag = np.arange(LAGS)[None, :] - (LAGS - 1) // 2
    angles = (2.0 * math.pi / seg_length) * (j * lag % seg_length)
    real, imag = np.cos(angles).astype(np.float32), -np.sin(angles).astype(np.float32)
    parts = []
    for h in range(FREQS // LANES):
        rows = slice(h * LANES, (h + 1) * LANES)
        parts += [real[rows], imag[rows]]
    return np.concatenate(parts, axis=0).astype(ml_dtypes.bfloat16)


TABLE_ROWS = 6144


def tables(seg_length):
    forward, inverse = forward_table(seg_length), inverse_table(seg_length)
    both = np.zeros((max(TABLE_ROWS, seg_length + 2 * FREQS), 2 * FREQS), ml_dtypes.bfloat16)
    both[:seg_length] = forward
    both[seg_length : seg_length + 2 * FREQS, :LAGS] = inverse
    return both


def accumulate(load, spectra, acc, count, first, share, block, fresh):
    halves = FREQS // LANES
    for n in range(count):
        for h in range(halves):
            wide = load(n, h).astype(jnp.float32)
            spectra[n, 2 * h] = wide[:, :LANES]
            spectra[n, 2 * h + 1] = wide[:, LANES:]

    def tile(r, _):
        here = pl.ds(pl.multiple_of(r * 8, 8), 8)
        for h in range(halves):
            re = slice(2 * h * LANES, (2 * h + 1) * LANES)
            im = slice((2 * h + 1) * LANES, (2 * h + 2) * LANES)
            a0 = [spectra[n, 2 * h, here, :] for n in range(count)]
            a1 = [spectra[n, 2 * h + 1, here, :] for n in range(count)]
            for k in range(share):
                at = pl.ds(pl.multiple_of(k * block + r * 8, 8), 8)
                there = pl.ds(first + (r * 8 + k + 1), 8)
                real = imag = None
                for n in range(count):
                    b0, b1 = spectra[n, 2 * h, there, :], spectra[n, 2 * h + 1, there, :]
                    x, y = a0[n] * b0 + a1[n] * b1, a1[n] * b0 - a0[n] * b1
                    real = x if real is None else real + x
                    imag = y if imag is None else imag + y
                acc[at, re] = real if fresh else acc[at, re] + real
                acc[at, im] = imag if fresh else acc[at, im] + imag
        return 0

    lax.fori_loop(0, block // 8, tile, 0)


def stack_kernel(
    nf, nt, nq, norm, x_hbm, table_hbm, out_ref,
    acc, x_ref, table_ref, inverse_ref, white, g_ref, spectra_ref,
    load_sem, fibre_send, tm_send, recv_sem, pair_send, pair_recv,
):
    fibre, tm, core = lax.axis_index("fibre"), lax.axis_index("tm"), lax.axis_index("freq")
    me = fibre * nt + tm
    sibling = {"freq": 1 - core}
    chans = x_ref.shape[0]
    block = chans // nf
    rows = block + OFFS
    chunks = 2
    part = rows // chunks
    step = 128
    steps = chans // step
    depth = table_ref.shape[0] // 4

    def load_x(i):
        here = pl.ds(pl.multiple_of(i * step, step), step)
        return pltpu.make_async_copy(x_hbm.at[0, here], x_ref.at[here], load_sem.at[5 + i])

    def load_table(i):
        here = pl.ds(i * depth, depth)
        return pltpu.make_async_copy(table_hbm.at[here], table_ref.at[here], load_sem.at[i])

    for i in range(4):
        load_table(i).start()
    for i in range(steps):
        load_x(i).start()
    load_inverse = pltpu.make_async_copy(
        table_hbm.at[pl.ds(table_ref.shape[0], 2 * FREQS)], inverse_ref, load_sem.at[4]
    )
    load_inverse.start()

    barrier = pltpu.get_barrier_semaphore()
    pl.semaphore_signal(barrier, inc=1, device_id=sibling, device_id_type=MESH)
    for i in range(1, nf):
        to = {"fibre": lax.rem(fibre + i, nf)}
        pl.semaphore_signal(barrier, inc=1, device_id=to, device_id_type=MESH)
    for i in range(1, nt):
        to = {"tm": lax.rem(tm + i, nt)}
        pl.semaphore_signal(barrier, inc=1, device_id=to, device_id_type=MESH)

    for i in range(4):
        load_table(i).wait()

    def whiten(i, _):
        here = pl.ds(pl.multiple_of(i * step, step), step)
        load_x(i).wait()
        spectra = jnp.dot(x_ref[here, :], table_ref[...], preferred_element_type=jnp.float32)
        squares = spectra * spectra
        power = jnp.sum(squares, axis=1, keepdims=True) * (1.0 / FREQS)
        floor = (power + 1e-06) * (water_level * water_level)
        for h in range(FREQS // LANES):
            re = slice(2 * h * LANES, (2 * h + 1) * LANES)
            im = slice((2 * h + 1) * LANES, (2 * h + 2) * LANES)
            scale = lax.rsqrt(jnp.maximum(squares[:, re] + squares[:, im], floor))
            white[h, here, 0:LANES] = (spectra[:, re] * scale).astype(jnp.bfloat16)
            white[h, here, LANES : 2 * LANES] = (spectra[:, im] * scale).astype(jnp.bfloat16)
        return 0

    white[:, chans:, :] = jnp.zeros((2, OFFS, 2 * LANES), jnp.bfloat16)
    lax.fori_loop(0, steps, whiten, 0, unroll=steps <= 4)

    pl.semaphore_wait(barrier, nf + nt - 1)

    def rows_of(f, c):
        return pl.ds(pl.multiple_of(f * block + c * part, 16), part)

    def landing(s, c):
        return g_ref.at[s, core, pl.ds(c * part, part)]

    def along_fibre(f, c):
        return pltpu.make_async_remote_copy(
            src_ref=white.at[core, rows_of(f, c)],
            dst_ref=landing(me, c),
            send_sem=fibre_send.at[f, c],
            recv_sem=recv_sem.at[me, c],
            device_id={"fibre": f},
            device_id_type=MESH,
        )

    def along_tm(f, i, c, own=False):
        s = f * nt + tm
        return pltpu.make_async_remote_copy(
            src_ref=white.at[core, rows_of(fibre, c)] if own else landing(s, c),
            dst_ref=landing(s, c),
            send_sem=tm_send.at[f, i, c],
            recv_sem=recv_sem.at[s, c],
            device_id={"tm": lax.rem(tm + i, nt)},
            device_id_type=MESH,
        )

    def arrived(s, c):
        return pltpu.make_async_remote_copy(
            src_ref=landing(s, c),
            dst_ref=landing(s, c),
            send_sem=pair_send.at[s],
            recv_sem=recv_sem.at[s, c],
            device_id=sibling,
            device_id_type=MESH,
        )

    def across(s, half):
        return pltpu.make_async_remote_copy(
            src_ref=g_ref.at[s, half],
            dst_ref=g_ref.at[s, half],
            send_sem=pair_send.at[s],
            recv_sem=pair_recv.at[s],
            device_id=sibling,
            device_id_type=MESH,
        )

    def loop(low, high, body):
        if high - low <= 8:
            for i in range(low, high):
                body(i)
        else:
            lax.fori_loop(low, high, lambda i, _: (body(i), 0)[1], 0)

    def nearest_first(body):
        def at_distance(d):
            for f in (fibre + d, fibre - d):
                pl.when(jnp.logical_and(f >= 0, f < nf))(functools.partial(body, f))

        loop(1, nf, at_distance)

    for c in range(chunks):
        for i in range(1, nt):
            along_tm(fibre, i, c, own=True).start()

    @nearest_first
    def _(f):
        for c in range(chunks):
            along_fibre(f, c).start()

    g_ref[me] = jnp.stack(
        [white[h, pl.ds(pl.multiple_of(fibre * block, 16), rows), :] for h in range(2)]
    )

    @nearest_first
    def _(f):
        s = f * nt + tm
        for c in range(chunks):
            arrived(s, c).wait_recv()
            for i in range(1, nt):
                along_tm(f, i, c).start()
        across(s, core).start()

    share = acc.shape[0] // block
    place = tm * nq + core
    first = place * share

    @nearest_first
    def _(f):
        across(f * nt + tm, 1 - core).wait_recv()

    def add(batch, index, fresh):
        def load(n, h):
            return g_ref[index(n), h]

        accumulate(load, spectra_ref, acc, batch, first, share, block, fresh)

    batch = math.gcd(nf, 4)
    add(batch, lambda n: n * nt + tm, True)
    if nf > batch:
        loop(1, nf // batch, lambda i: add(batch, lambda n: (i * batch + n) * nt + tm, False))

    def pass_on(f):
        for i in range(1, nt):
            s = f * nt + lax.rem(tm + i, nt)
            for c in range(chunks):
                arrived(s, c).wait_recv()
            across(s, core).start()

    pass_on(fibre)
    nearest_first(pass_on)
    for i in range(1, nt):
        other = lax.rem(tm + i, nt)

        def part_of(b):
            for n in range(batch):
                across((b * batch + n) * nt + other, 1 - core).wait_recv()
            add(batch, lambda n: (b * batch + n) * nt + other, False)

        loop(0, nf // batch, part_of)

    load_inverse.wait()
    group = 4
    for k in range(share // group):
        here = slice(k * group * block, (k + 1) * group * block)
        terms = jnp.dot(
            acc[here, :].astype(jnp.bfloat16), inverse_ref[...], preferred_element_type=jnp.float32
        )
        out_ref[k * group : (k + 1) * group] = (terms[:, :LAGS] * norm).reshape(group, block, LAGS)

    for i in range(1, nt):
        across(fibre * nt + lax.rem(tm + i, nt), core).wait_send()
        for c in range(chunks):
            along_tm(fibre, i, c, own=True).wait_send()

    @nearest_first
    def _(f):
        for c in range(chunks):
            along_fibre(f, c).wait_send()
        for i in range(nt):
            across(f * nt + lax.rem(tm + i, nt), core).wait_send()
            if i > 0:
                for c in range(chunks):
                    along_tm(f, i, c).wait_send()


def local(nf, nt, nq, strain_rate):
    _, chans, seg_length = strain_rate.shape
    segs = nf * nt
    block = chans // nf
    rows = block + OFFS
    share = OFFS // (nt * nq)
    norm = 1.0 / math.sqrt(segs * FREQS)
    vmem = pl.BlockSpec(memory_space=pltpu.VMEM)
    return pl.pallas_call(
        functools.partial(stack_kernel, nf, nt, nq, norm),
        out_shape=jax.ShapeDtypeStruct((share, block, LAGS), jnp.float32),
        in_specs=[pl.BlockSpec(memory_space=pltpu.HBM)] * 2,
        out_specs=vmem,
        scratch_shapes=[
            pltpu.VMEM((share * block, 2 * FREQS), jnp.float32),
            pltpu.VMEM((chans, seg_length), jnp.bfloat16),
            pltpu.VMEM((seg_length, 2 * FREQS), jnp.bfloat16),
            pltpu.VMEM((2 * FREQS, 2 * FREQS), jnp.bfloat16),
            pltpu.VMEM((2, chans + OFFS, 2 * LANES), jnp.bfloat16),
            pltpu.VMEM((segs, 2, rows, 2 * LANES), jnp.bfloat16),
            pltpu.VMEM((math.gcd(nf, 4), 4, rows, LANES), jnp.float32),
            pltpu.SemaphoreType.DMA((5 + chans // 128,)),
            pltpu.SemaphoreType.DMA((nf, 2)),
            pltpu.SemaphoreType.DMA((nf, nt, 2)),
            pltpu.SemaphoreType.DMA((segs, 2)),
            pltpu.SemaphoreType.DMA((segs,)),
            pltpu.SemaphoreType.DMA((segs,)),
        ],
        compiler_params=pltpu.CompilerParams(
            collective_id=0, has_side_effects=True, vmem_limit_bytes=50 << 20
        ),
    )(strain_rate, jnp.asarray(tables(seg_length)))


def solution(mesh):
    sizes = mesh.shape
    return jax.shard_map(
        functools.partial(local, sizes["fibre"], sizes["tm"], sizes["freq"]),
        mesh=mesh,
        in_specs=(P(("fibre", "tm"), "groups", None),),
        out_specs=P(("tm", "freq"), ("groups", "fibre"), None),
        check_vma=False,
    )
```

```python
import functools
import math

import jax
import jax.numpy as jnp
import numpy as np
from jax import lax
from jax.experimental import pallas as pl
from jax.experimental.pallas import tpu as pltpu
from jax.sharding import PartitionSpec as P
import ml_dtypes

FREQS = 256
OFFS = 64
LAGS = 401
LANES = 128
MESH = pl.DeviceIdType.MESH

water_level = 0.5


def forward_table(seg_length):
    t = np.arange(seg_length)[:, None]
    j = np.arange(1, FREQS + 1)[None, :]
    angles = (2.0 * math.pi / seg_length) * (t * j % seg_length)
    taper = 0.5 - 0.5 * np.cos(2.0 * math.pi / seg_length * t)
    real = (taper * np.cos(angles)).astype(np.float32)
    imag = (-taper * np.sin(angles)).astype(np.float32)
    parts = []
    for h in range(FREQS // LANES):
        cols = slice(h * LANES, (h + 1) * LANES)
        parts += [real[:, cols], imag[:, cols]]
    return np.concatenate(parts, axis=1).astype(ml_dtypes.bfloat16)


def inverse_table(seg_length):
    j = np.arange(1, FREQS + 1)[:, None]
    lag = np.arange(LAGS)[None, :] - (LAGS - 1) // 2
    angles = (2.0 * math.pi / seg_length) * (j * lag % seg_length)
    real, imag = np.cos(angles).astype(np.float32), -np.sin(angles).astype(np.float32)
    parts = []
    for h in range(FREQS // LANES):
        rows = slice(h * LANES, (h + 1) * LANES)
        parts += [real[rows], imag[rows]]
    return np.concatenate(parts, axis=0).astype(ml_dtypes.bfloat16)


TABLE_ROWS = 6144


def tables(seg_length):
    forward, inverse = forward_table(seg_length), inverse_table(seg_length)
    both = np.zeros((max(TABLE_ROWS, seg_length + 2 * FREQS), 2 * FREQS), ml_dtypes.bfloat16)
    both[:seg_length] = forward
    both[seg_length : seg_length + 2 * FREQS, :LAGS] = inverse
    return both


def accumulate(load, spectra, acc, count, first, share, block, fresh):
    halves = FREQS // LANES
    for n in range(count):
        for h in range(halves):
            wide = load(n, h).astype(jnp.float32)
            spectra[n, 2 * h] = wide[:, :LANES]
            spectra[n, 2 * h + 1] = wide[:, LANES:]

    def tile(r, _):
        here = pl.ds(pl.multiple_of(r * 8, 8), 8)
        for h in range(halves):
            re = slice(2 * h * LANES, (2 * h + 1) * LANES)
            im = slice((2 * h + 1) * LANES, (2 * h + 2) * LANES)
            a0 = [spectra[n, 2 * h, here, :] for n in range(count)]
            a1 = [spectra[n, 2 * h + 1, here, :] for n in range(count)]
            for k in range(share):
                at = pl.ds(pl.multiple_of(k * block + r * 8, 8), 8)
                there = pl.ds(first + (r * 8 + k + 1), 8)
                real = imag = None
                for n in range(count):
                    b0, b1 = spectra[n, 2 * h, there, :], spectra[n, 2 * h + 1, there, :]
                    x, y = a0[n] * b0 + a1[n] * b1, a1[n] * b0 - a0[n] * b1
                    real = x if real is None else real + x
                    imag = y if imag is None else imag + y
                acc[at, re] = real if fresh else acc[at, re] + real
                acc[at, im] = imag if fresh else acc[at, im] + imag
        return 0

    lax.fori_loop(0, block // 8, tile, 0)


def stack_kernel(
    nf, nt, nq, norm, x_hbm, table_hbm, out_ref,
    acc, x_ref, table_ref, inverse_ref, white, g_ref, spectra_ref,
    load_sem, fibre_send, tm_send, recv_sem, pair_send, pair_recv,
):
    fibre, tm, core = lax.axis_index("fibre"), lax.axis_index("tm"), lax.axis_index("freq")
    me = fibre * nt + tm
    sibling = {"freq": 1 - core}
    chans = x_ref.shape[0]
    block = chans // nf
    rows = block + OFFS
    chunks = 2
    part = rows // chunks
    step = 128
    steps = chans // step
    depth = table_ref.shape[0] // 4

    def load_x(i):
        here = pl.ds(pl.multiple_of(i * step, step), step)
        return pltpu.make_async_copy(x_hbm.at[0, here], x_ref.at[here], load_sem.at[5 + i])

    def load_table(i):
        here = pl.ds(i * depth, depth)
        return pltpu.make_async_copy(table_hbm.at[here], table_ref.at[here], load_sem.at[i])

    for i in range(4):
        load_table(i).start()
    for i in range(steps):
        load_x(i).start()
    load_inverse = pltpu.make_async_copy(
        table_hbm.at[pl.ds(table_ref.shape[0], 2 * FREQS)], inverse_ref, load_sem.at[4]
    )
    load_inverse.start()

    barrier = pltpu.get_barrier_semaphore()
    pl.semaphore_signal(barrier, inc=1, device_id=sibling, device_id_type=MESH)
    for i in range(1, nf):
        to = {"fibre": lax.rem(fibre + i, nf)}
        pl.semaphore_signal(barrier, inc=1, device_id=to, device_id_type=MESH)
    for i in range(1, nt):
        to = {"tm": lax.rem(tm + i, nt)}
        pl.semaphore_signal(barrier, inc=1, device_id=to, device_id_type=MESH)

    for i in range(4):
        load_table(i).wait()

    def whiten(i, _):
        here = pl.ds(pl.multiple_of(i * step, step), step)
        load_x(i).wait()
        spectra = jnp.dot(x_ref[here, :], table_ref[...], preferred_element_type=jnp.float32)
        squares = spectra * spectra
        power = jnp.sum(squares, axis=1, keepdims=True) * (1.0 / FREQS)
        floor = (power + 1e-06) * (water_level * water_level)
        for h in range(FREQS // LANES):
            re = slice(2 * h * LANES, (2 * h + 1) * LANES)
            im = slice((2 * h + 1) * LANES, (2 * h + 2) * LANES)
            scale = lax.rsqrt(jnp.maximum(squares[:, re] + squares[:, im], floor))
            white[h, here, 0:LANES] = (spectra[:, re] * scale).astype(jnp.bfloat16)
            white[h, here, LANES : 2 * LANES] = (spectra[:, im] * scale).astype(jnp.bfloat16)
        return 0

    white[:, chans:, :] = jnp.zeros((2, OFFS, 2 * LANES), jnp.bfloat16)
    lax.fori_loop(0, steps, whiten, 0, unroll=steps <= 4)

    pl.semaphore_wait(barrier, nf + nt - 1)

    def rows_of(f, c):
        return pl.ds(pl.multiple_of(f * block + c * part, 16), part)

    def landing(s, c):
        return g_ref.at[s, core, pl.ds(c * part, part)]

    def along_fibre(f, c):
        return pltpu.make_async_remote_copy(
            src_ref=white.at[core, rows_of(f, c)],
            dst_ref=landing(me, c),
            send_sem=fibre_send.at[f, c],
            recv_sem=recv_sem.at[me, c],
            device_id={"fibre": f},
            device_id_type=MESH,
        )

    def along_tm(f, i, c, own=False):
        s = f * nt + tm
        return pltpu.make_async_remote_copy(
            src_ref=white.at[core, rows_of(fibre, c)] if own else landing(s, c),
            dst_ref=landing(s, c),
            send_sem=tm_send.at[f, i, c],
            recv_sem=recv_sem.at[s, c],
            device_id={"tm": lax.rem(tm + i, nt)},
            device_id_type=MESH,
        )

    def arrived(s, c):
        return pltpu.make_async_remote_copy(
            src_ref=landing(s, c),
            dst_ref=landing(s, c),
            send_sem=pair_send.at[s],
            recv_sem=recv_sem.at[s, c],
            device_id=sibling,
            device_id_type=MESH,
        )

    def across(s, half):
        return pltpu.make_async_remote_copy(
            src_ref=g_ref.at[s, half],
            dst_ref=g_ref.at[s, half],
            send_sem=pair_send.at[s],
            recv_sem=pair_recv.at[s],
            device_id=sibling,
            device_id_type=MESH,
        )

    def loop(low, high, body):
        if high - low <= 8:
            for i in range(low, high):
                body(i)
        else:
            lax.fori_loop(low, high, lambda i, _: (body(i), 0)[1], 0)

    def nearest_first(body):
        def at_distance(d):
            for f in (fibre + d, fibre - d):
                pl.when(jnp.logical_and(f >= 0, f < nf))(functools.partial(body, f))

        loop(1, nf, at_distance)

    for c in range(chunks):
        for i in range(1, nt):
            along_tm(fibre, i, c, own=True).start()

    def send_rows(d):
        for f in (fibre + d, fibre - d):

            @pl.when(jnp.logical_and(f >= 0, f < nf))
            def _(f=f):
                for c in range(chunks):
                    along_fibre(f, c).start()

    loop(1, nf, lambda i: send_rows(nf - i))

    g_ref[me] = jnp.stack(
        [white[h, pl.ds(pl.multiple_of(fibre * block, 16), rows), :] for h in range(2)]
    )

    @nearest_first
    def _(f):
        s = f * nt + tm
        for c in range(chunks):
            arrived(s, c).wait_recv()
            for i in range(1, nt):
                along_tm(f, i, c).start()
        across(s, core).start()

    share = acc.shape[0] // block
    place = tm * nq + core
    first = place * share

    @nearest_first
    def _(f):
        across(f * nt + tm, 1 - core).wait_recv()

    def add(batch, index, fresh):
        def load(n, h):
            return g_ref[index(n), h]

        accumulate(load, spectra_ref, acc, batch, first, share, block, fresh)

    batch = math.gcd(nf, 4)
    add(batch, lambda n: n * nt + tm, True)
    if nf > batch:
        loop(1, nf // batch, lambda i: add(batch, lambda n: (i * batch + n) * nt + tm, False))

    def pass_on(f):
        for i in range(1, nt):
            s = f * nt + lax.rem(tm + i, nt)
            for c in range(chunks):
                arrived(s, c).wait_recv()
            across(s, core).start()

    pass_on(fibre)
    nearest_first(pass_on)
    for i in range(1, nt):
        other = lax.rem(tm + i, nt)

        def part_of(b):
            for n in range(batch):
                across((b * batch + n) * nt + other, 1 - core).wait_recv()
            add(batch, lambda n: (b * batch + n) * nt + other, False)

        loop(0, nf // batch, part_of)

    load_inverse.wait()
    group = 4
    for k in range(share // group):
        here = slice(k * group * block, (k + 1) * group * block)
        terms = jnp.dot(
            acc[here, :].astype(jnp.bfloat16), inverse_ref[...], preferred_element_type=jnp.float32
        )
        out_ref[k * group : (k + 1) * group] = (terms[:, :LAGS] * norm).reshape(group, block, LAGS)

    for i in range(1, nt):
        across(fibre * nt + lax.rem(tm + i, nt), core).wait_send()
        for c in range(chunks):
            along_tm(fibre, i, c, own=True).wait_send()

    @nearest_first
    def _(f):
        for c in range(chunks):
            along_fibre(f, c).wait_send()
        for i in range(nt):
            across(f * nt + lax.rem(tm + i, nt), core).wait_send()
            if i > 0:
                for c in range(chunks):
                    along_tm(f, i, c).wait_send()


def local(nf, nt, nq, strain_rate):
    _, chans, seg_length = strain_rate.shape
    segs = nf * nt
    block = chans // nf
    rows = block + OFFS
    share = OFFS // (nt * nq)
    norm = 1.0 / math.sqrt(segs * FREQS)
    vmem = pl.BlockSpec(memory_space=pltpu.VMEM)
    return pl.pallas_call(
        functools.partial(stack_kernel, nf, nt, nq, norm),
        out_shape=jax.ShapeDtypeStruct((share, block, LAGS), jnp.float32),
        in_specs=[pl.BlockSpec(memory_space=pltpu.HBM)] * 2,
        out_specs=vmem,
        scratch_shapes=[
            pltpu.VMEM((share * block, 2 * FREQS), jnp.float32),
            pltpu.VMEM((chans, seg_length), jnp.bfloat16),
            pltpu.VMEM((seg_length, 2 * FREQS), jnp.bfloat16),
            pltpu.VMEM((2 * FREQS, 2 * FREQS), jnp.bfloat16),
            pltpu.VMEM((2, chans + OFFS, 2 * LANES), jnp.bfloat16),
            pltpu.VMEM((segs, 2, rows, 2 * LANES), jnp.bfloat16),
            pltpu.VMEM((math.gcd(nf, 4), 4, rows, LANES), jnp.float32),
            pltpu.SemaphoreType.DMA((5 + chans // 128,)),
            pltpu.SemaphoreType.DMA((nf, 2)),
            pltpu.SemaphoreType.DMA((nf, nt, 2)),
            pltpu.SemaphoreType.DMA((segs, 2)),
            pltpu.SemaphoreType.DMA((segs,)),
            pltpu.SemaphoreType.DMA((segs,)),
        ],
        compiler_params=pltpu.CompilerParams(
            collective_id=0, has_side_effects=True, vmem_limit_bytes=50 << 20
        ),
    )(strain_rate, jnp.asarray(tables(seg_length)))


def solution(mesh):
    sizes = mesh.shape
    return jax.shard_map(
        functools.partial(local, sizes["fibre"], sizes["tm"], sizes["freq"]),
        mesh=mesh,
        in_specs=(P(("fibre", "tm"), "groups", None),),
        out_specs=P(("tm", "freq"), ("groups", "fibre"), None),
        check_vma=False,
    )
```

```python
import functools
import math

import jax
import jax.numpy as jnp
import numpy as np
from jax import lax
from jax.experimental import pallas as pl
from jax.experimental.pallas import tpu as pltpu
from jax.sharding import PartitionSpec as P
import ml_dtypes

FREQS = 256
OFFS = 64
LAGS = 401
LANES = 128
MESH = pl.DeviceIdType.MESH

water_level = 0.5


def forward_table(seg_length):
    t = np.arange(seg_length)[:, None]
    j = np.arange(1, FREQS + 1)[None, :]
    angles = (2.0 * math.pi / seg_length) * (t * j % seg_length)
    taper = 0.5 - 0.5 * np.cos(2.0 * math.pi / seg_length * t)
    real = (taper * np.cos(angles)).astype(np.float32)
    imag = (-taper * np.sin(angles)).astype(np.float32)
    parts = []
    for h in range(FREQS // LANES):
        cols = slice(h * LANES, (h + 1) * LANES)
        parts += [real[:, cols], imag[:, cols]]
    return np.concatenate(parts, axis=1).astype(ml_dtypes.bfloat16)


def inverse_table(seg_length):
    j = np.arange(1, FREQS + 1)[:, None]
    lag = np.arange(LAGS)[None, :] - (LAGS - 1) // 2
    angles = (2.0 * math.pi / seg_length) * (j * lag % seg_length)
    real, imag = np.cos(angles).astype(np.float32), -np.sin(angles).astype(np.float32)
    parts = []
    for h in range(FREQS // LANES):
        rows = slice(h * LANES, (h + 1) * LANES)
        parts += [real[rows], imag[rows]]
    return np.concatenate(parts, axis=0).astype(ml_dtypes.bfloat16)


TABLE_ROWS = 6144


def tables(seg_length):
    forward, inverse = forward_table(seg_length), inverse_table(seg_length)
    both = np.zeros((max(TABLE_ROWS, seg_length + 2 * FREQS), 2 * FREQS), ml_dtypes.bfloat16)
    both[:seg_length] = forward
    both[seg_length : seg_length + 2 * FREQS, :LAGS] = inverse
    return both


def accumulate(load, spectra, acc, count, first, share, block, fresh):
    halves = FREQS // LANES
    for n in range(count):
        for h in range(halves):
            wide = load(n, h).astype(jnp.float32)
            spectra[n, 2 * h] = wide[:, :LANES]
            spectra[n, 2 * h + 1] = wide[:, LANES:]

    def tile(r, _):
        here = pl.ds(pl.multiple_of(r * 8, 8), 8)
        for h in range(halves):
            re = slice(2 * h * LANES, (2 * h + 1) * LANES)
            im = slice((2 * h + 1) * LANES, (2 * h + 2) * LANES)
            a0 = [spectra[n, 2 * h, here, :] for n in range(count)]
            a1 = [spectra[n, 2 * h + 1, here, :] for n in range(count)]
            for k in range(share):
                at = pl.ds(pl.multiple_of(k * block + r * 8, 8), 8)
                there = pl.ds(first + (r * 8 + k + 1), 8)
                real = imag = None
                for n in range(count):
                    b0, b1 = spectra[n, 2 * h, there, :], spectra[n, 2 * h + 1, there, :]
                    x, y = a0[n] * b0 + a1[n] * b1, a1[n] * b0 - a0[n] * b1
                    real = x if real is None else real + x
                    imag = y if imag is None else imag + y
                acc[at, re] = real if fresh else acc[at, re] + real
                acc[at, im] = imag if fresh else acc[at, im] + imag
        return 0

    lax.fori_loop(0, block // 8, tile, 0)


def stack_kernel(
    nf, nt, nq, norm, x_hbm, table_hbm, out_ref,
    acc, x_ref, table_ref, inverse_ref, white, g_ref, spectra_ref,
    load_sem, fibre_send, tm_send, recv_sem, pair_send, pair_recv,
):
    fibre, tm, core = lax.axis_index("fibre"), lax.axis_index("tm"), lax.axis_index("freq")
    me = fibre * nt + tm
    sibling = {"freq": 1 - core}
    chans = x_ref.shape[0]
    block = chans // nf
    rows = block + OFFS
    chunks = 4
    part = rows // chunks
    step = 128
    steps = chans // step
    depth = table_ref.shape[0] // 4

    def load_x(i):
        here = pl.ds(pl.multiple_of(i * step, step), step)
        return pltpu.make_async_copy(x_hbm.at[0, here], x_ref.at[here], load_sem.at[5 + i])

    def load_table(i):
        here = pl.ds(i * depth, depth)
        return pltpu.make_async_copy(table_hbm.at[here], table_ref.at[here], load_sem.at[i])

    for i in range(4):
        load_table(i).start()
    for i in range(steps):
        load_x(i).start()
    load_inverse = pltpu.make_async_copy(
        table_hbm.at[pl.ds(table_ref.shape[0], 2 * FREQS)], inverse_ref, load_sem.at[4]
    )
    load_inverse.start()

    barrier = pltpu.get_barrier_semaphore()
    pl.semaphore_signal(barrier, inc=1, device_id=sibling, device_id_type=MESH)
    for i in range(1, nf):
        to = {"fibre": lax.rem(fibre + i, nf)}
        pl.semaphore_signal(barrier, inc=1, device_id=to, device_id_type=MESH)
    for i in range(1, nt):
        to = {"tm": lax.rem(tm + i, nt)}
        pl.semaphore_signal(barrier, inc=1, device_id=to, device_id_type=MESH)

    for i in range(4):
        load_table(i).wait()

    def whiten(i, _):
        here = pl.ds(pl.multiple_of(i * step, step), step)
        load_x(i).wait()
        spectra = jnp.dot(x_ref[here, :], table_ref[...], preferred_element_type=jnp.float32)
        squares = spectra * spectra
        power = jnp.sum(squares, axis=1, keepdims=True) * (1.0 / FREQS)
        floor = (power + 1e-06) * (water_level * water_level)
        for h in range(FREQS // LANES):
            re = slice(2 * h * LANES, (2 * h + 1) * LANES)
            im = slice((2 * h + 1) * LANES, (2 * h + 2) * LANES)
            scale = lax.rsqrt(jnp.maximum(squares[:, re] + squares[:, im], floor))
            white[h, here, 0:LANES] = (spectra[:, re] * scale).astype(jnp.bfloat16)
            white[h, here, LANES : 2 * LANES] = (spectra[:, im] * scale).astype(jnp.bfloat16)
        return 0

    white[:, chans:, :] = jnp.zeros((2, OFFS, 2 * LANES), jnp.bfloat16)
    lax.fori_loop(0, steps, whiten, 0, unroll=steps <= 4)

    pl.semaphore_wait(barrier, nf + nt - 1)

    def rows_of(f, c):
        return pl.ds(pl.multiple_of(f * block + c * part, 16), part)

    def landing(s, c):
        return g_ref.at[s, core, pl.ds(c * part, part)]

    def along_fibre(f, c):
        return pltpu.make_async_remote_copy(
            src_ref=white.at[core, rows_of(f, c)],
            dst_ref=landing(me, c),
            send_sem=fibre_send.at[f, c],
            recv_sem=recv_sem.at[me, c],
            device_id={"fibre": f},
            device_id_type=MESH,
        )

    def along_tm(f, i, c, own=False):
        s = f * nt + tm
        return pltpu.make_async_remote_copy(
            src_ref=white.at[core, rows_of(fibre, c)] if own else landing(s, c),
            dst_ref=landing(s, c),
            send_sem=tm_send.at[f, i, c],
            recv_sem=recv_sem.at[s, c],
            device_id={"tm": lax.rem(tm + i, nt)},
            device_id_type=MESH,
        )

    def arrived(s, c):
        return pltpu.make_async_remote_copy(
            src_ref=landing(s, c),
            dst_ref=landing(s, c),
            send_sem=pair_send.at[s],
            recv_sem=recv_sem.at[s, c],
            device_id=sibling,
            device_id_type=MESH,
        )

    def across(s, half):
        return pltpu.make_async_remote_copy(
            src_ref=g_ref.at[s, half],
            dst_ref=g_ref.at[s, half],
            send_sem=pair_send.at[s],
            recv_sem=pair_recv.at[s],
            device_id=sibling,
            device_id_type=MESH,
        )

    def loop(low, high, body):
        if high - low <= 8:
            for i in range(low, high):
                body(i)
        else:
            lax.fori_loop(low, high, lambda i, _: (body(i), 0)[1], 0)

    def nearest_first(body):
        def at_distance(d):
            for f in (fibre + d, fibre - d):
                pl.when(jnp.logical_and(f >= 0, f < nf))(functools.partial(body, f))

        loop(1, nf, at_distance)

    for c in range(chunks):
        for i in range(1, nt):
            along_tm(fibre, i, c, own=True).start()

    def send_rows(d):
        for f in (fibre + d, fibre - d):

            @pl.when(jnp.logical_and(f >= 0, f < nf))
            def _(f=f):
                for c in range(chunks):
                    along_fibre(f, c).start()

    loop(1, nf, lambda i: send_rows(nf - i))

    g_ref[me] = jnp.stack(
        [white[h, pl.ds(pl.multiple_of(fibre * block, 16), rows), :] for h in range(2)]
    )

    @nearest_first
    def _(f):
        s = f * nt + tm
        for c in range(chunks):
            arrived(s, c).wait_recv()
            for i in range(1, nt):
                along_tm(f, i, c).start()
        across(s, core).start()

    share = acc.shape[0] // block
    place = tm * nq + core
    first = place * share

    @nearest_first
    def _(f):
        across(f * nt + tm, 1 - core).wait_recv()

    def add(batch, index, fresh):
        def load(n, h):
            return g_ref[index(n), h]

        accumulate(load, spectra_ref, acc, batch, first, share, block, fresh)

    batch = math.gcd(nf, 4)
    add(batch, lambda n: n * nt + tm, True)
    if nf > batch:
        loop(1, nf // batch, lambda i: add(batch, lambda n: (i * batch + n) * nt + tm, False))

    def pass_on(f):
        for i in range(1, nt):
            s = f * nt + lax.rem(tm + i, nt)
            for c in range(chunks):
                arrived(s, c).wait_recv()
            across(s, core).start()

    pass_on(fibre)
    nearest_first(pass_on)
    for i in range(1, nt):
        other = lax.rem(tm + i, nt)

        def part_of(b):
            for n in range(batch):
                across((b * batch + n) * nt + other, 1 - core).wait_recv()
            add(batch, lambda n: (b * batch + n) * nt + other, False)

        loop(0, nf // batch, part_of)

    load_inverse.wait()
    group = 4
    for k in range(share // group):
        here = slice(k * group * block, (k + 1) * group * block)
        terms = jnp.dot(
            acc[here, :].astype(jnp.bfloat16), inverse_ref[...], preferred_element_type=jnp.float32
        )
        out_ref[k * group : (k + 1) * group] = (terms[:, :LAGS] * norm).reshape(group, block, LAGS)

    for i in range(1, nt):
        across(fibre * nt + lax.rem(tm + i, nt), core).wait_send()
        for c in range(chunks):
            along_tm(fibre, i, c, own=True).wait_send()

    @nearest_first
    def _(f):
        for c in range(chunks):
            along_fibre(f, c).wait_send()
        for i in range(nt):
            across(f * nt + lax.rem(tm + i, nt), core).wait_send()
            if i > 0:
                for c in range(chunks):
                    along_tm(f, i, c).wait_send()


def local(nf, nt, nq, strain_rate):
    _, chans, seg_length = strain_rate.shape
    segs = nf * nt
    block = chans // nf
    rows = block + OFFS
    share = OFFS // (nt * nq)
    norm = 1.0 / math.sqrt(segs * FREQS)
    vmem = pl.BlockSpec(memory_space=pltpu.VMEM)
    return pl.pallas_call(
        functools.partial(stack_kernel, nf, nt, nq, norm),
        out_shape=jax.ShapeDtypeStruct((share, block, LAGS), jnp.float32),
        in_specs=[pl.BlockSpec(memory_space=pltpu.HBM)] * 2,
        out_specs=vmem,
        scratch_shapes=[
            pltpu.VMEM((share * block, 2 * FREQS), jnp.float32),
            pltpu.VMEM((chans, seg_length), jnp.bfloat16),
            pltpu.VMEM((seg_length, 2 * FREQS), jnp.bfloat16),
            pltpu.VMEM((2 * FREQS, 2 * FREQS), jnp.bfloat16),
            pltpu.VMEM((2, chans + OFFS, 2 * LANES), jnp.bfloat16),
            pltpu.VMEM((segs, 2, rows, 2 * LANES), jnp.bfloat16),
            pltpu.VMEM((math.gcd(nf, 4), 4, rows, LANES), jnp.float32),
            pltpu.SemaphoreType.DMA((5 + chans // 128,)),
            pltpu.SemaphoreType.DMA((nf, 4)),
            pltpu.SemaphoreType.DMA((nf, nt, 4)),
            pltpu.SemaphoreType.DMA((segs, 4)),
            pltpu.SemaphoreType.DMA((segs,)),
            pltpu.SemaphoreType.DMA((segs,)),
        ],
        compiler_params=pltpu.CompilerParams(
            collective_id=0, has_side_effects=True, vmem_limit_bytes=50 << 20
        ),
    )(strain_rate, jnp.asarray(tables(seg_length)))


def solution(mesh):
    sizes = mesh.shape
    return jax.shard_map(
        functools.partial(local, sizes["fibre"], sizes["tm"], sizes["freq"]),
        mesh=mesh,
        in_specs=(P(("fibre", "tm"), "groups", None),),
        out_specs=P(("tm", "freq"), ("groups", "fibre"), None),
        check_vma=False,
    )
```
